768 devices in a mesh: row: 16 (over z_lo, x), col: 48 (over z_hi, y, core).
Axes of the slice: x: 4, y: 8, z: 12 (z_hi: 3, z_lo: 4; z = z_hi * 4 + z_lo), core: 2. Of those that a mesh axis runs over, the one named last changes fastest.
Arguments:
- stored: float32 [4096, 12288], P('row', 'col'), may hold values from -6 to 6
- destination: int32 [4096], P('row'), may hold values from 0 to 4095, as said below
- tile_mask: int32 [16, 48], replicated, may hold values from 0 to 1, as said below
- integrals: bfloat16 [12288, 12288], P('row', 'col'), may hold values from -0.0546875 to 0.0546875
- denominators: float32 [4096, 12288], P('row', 'col'), may hold values from 0.5 to 4
Outputs:
- residual: float32 [4096, 12288], P('row', 'col')
The draws below stay inside these ranges and needn't reach their ends.
Inputs may be any that keep to these rules, and one draw needn't show every extreme that they name: destination is a permutation of the 4096 occupied pairs; the rows of each aligned block of 256 stored rows name exactly 16 occupied pairs in each aligned block of 256 occupied pairs. In every row of tile_mask, tile columns t and t + 1, for every even t, hold one 1 and one 0; so each row holds exactly 24 ones.
All inputs are finite; a program needn't handle non-finite values.
Results may differ from the reference program's by a relative error of at most 0.0029.
Values may be sent and summed in bfloat16 or wider, within the bound.
A program may use at most 32 MiB of HBM per device.

```python
import math
import jax
import jax.numpy as jnp

TILE = 256
KT = 48
ROWS_DEV = 256
VPAIRS = 12288
OPAIRS = 4096
TPD = 1


def permute_many(seed_key, count, length):

    def single(one_key):
        return jax.random.permutation(one_key, length)
    return jax.vmap(single)(jax.random.split(seed_key, count))


def draw_destination(key, part):
    key = jax.random.fold_in(key, 11)
    block_count = OPAIRS // ROWS_DEV
    share = ROWS_DEV // block_count
    source_key, target_key = jax.random.split(key)
    source_perm = permute_many(source_key, block_count, ROWS_DEV).astype(jnp.int32)
    target_perm = permute_many(target_key, block_count, ROWS_DEV).astype(jnp.int32)
    position = jnp.arange(ROWS_DEV, dtype=jnp.int32)
    target_block = position // share
    within = position % share
    source = jnp.arange(block_count, dtype=jnp.int32)[:, None]
    local_slot = target_perm[target_block[None, :], source * share + within[None, :]]
    target = target_block[None, :] * ROWS_DEV + local_slot
    row_index = source * ROWS_DEV + source_perm
    result = jnp.zeros((OPAIRS,), jnp.int32)
    return result.at[row_index.reshape(-1)].set(target.reshape(-1).astype(jnp.int32))


def draw_tile_mask(key, part):
    key = jax.random.fold_in(key, 23)
    tile_rows = OPAIRS // TILE
    bits = jax.random.randint(key, (tile_rows, KT // (2 * TPD), 1, TPD), 0, 2).astype(jnp.int32)
    paired = jnp.concatenate([bits, 1 - bits], axis=2)
    return paired.reshape(tile_rows, KT).astype(jnp.int32)


def shard_levels(key, extent, pieces, smallest, top_value):
    loudness, own = 1.0, jax.random.fold_in(key, 6)
    for dim, shards_of in pieces:
        steps = jnp.exp(jax.random.uniform(jax.random.fold_in(own, dim), (shards_of,), jnp.float32, smallest / len(pieces), top_value / len(pieces)))
        loudness = loudness * jnp.repeat(steps, extent[dim] // shards_of).reshape([-1 if axis == dim else 1 for axis in range(len(extent))])
    return loudness


def centred(own_key, extent, spread, bound, cuts=(), kind=jnp.bfloat16):
    gain = shard_levels(own_key, extent, cuts, -0.22, 0.18) if cuts else 1.0
    entries = jax.random.normal(own_key, extent, jnp.float32) * spread * gain
    return jnp.minimum(jnp.maximum(entries, -bound), bound).astype(kind)


def setup_inputs(seed: int = 0) -> dict:
    key_of = jax.random.split(jax.random.key(seed), 6)
    return {
        "stored": centred(key_of[0], (OPAIRS, VPAIRS), 1.0, 6.0, ((0, 16), (1, 48)), jnp.float32),
        "destination": draw_destination(jax.random.fold_in(key_of[5], 71), 0),
        "tile_mask": draw_tile_mask(jax.random.fold_in(key_of[5], 71), 0),
        "integrals": centred(key_of[3], (VPAIRS, VPAIRS), VPAIRS ** -0.5, 0.0546875, ((0, 16), (1, 48))),
        "denominators": jnp.clip(jnp.exp(math.log(4.0) - 2.0794415 * jax.random.uniform(key_of[4], (OPAIRS, VPAIRS), jnp.float32) ** shard_levels(key_of[4], (OPAIRS, VPAIRS), ((0, 16), (1, 48)), -0.2, 0.2)), 0.5, 4.0),
    }


def reference(stored, destination, tile_mask, integrals, denominators):
    placed = jnp.zeros_like(stored).at[destination].set(stored)
    full_mask = jnp.repeat(jnp.repeat(tile_mask, TILE, axis=0), TILE, axis=1)
    amplitudes = jnp.where(full_mask > 0, placed, jnp.zeros_like(placed)).astype(jnp.bfloat16)
    ladder = jnp.dot(amplitudes, integrals, preferred_element_type=jnp.float32)
    return ladder / denominators
```

```python
import jax
import jax.numpy as jnp
from jax import lax
from jax.experimental import pallas as pl
from jax.experimental.pallas import tpu as pltpu
from jax.sharding import PartitionSpec as P

MESH = pl.DeviceIdType.MESH
BF, F32, I32 = jnp.bfloat16, jnp.float32, jnp.int32
NX, NY, NZL, NZH = 4, 8, 4, 3
T = 256
KB = 768
HB = KB // 2
NP = 6
ORDER = [
    (0, 0), (1, 0), (0, 1), (1, 1), (2, 0), (0, 2), (1, 2), (2, 1), (3, 0), (0, 3), (1, 3), (2, 2), (3, 1),
    (0, 4), "B", (0, None), (1, 4), (2, 3), (3, 2), (1, None), (2, 4), (3, 3), (2, None), (3, 4), (3, None),
]


def iota(shape, dim):
    return lax.broadcasted_iota(I32, shape, dim)


def kernel(
    stored, dest, mask, b_hbm, den, out,
    t_ref, sib, merged, a_ref, b_ref, c_tx, c_rx, slots, w_ref,
    sib_s, a1_s, a_s, a_r, b_s, b_r, bs_s, bs_r, bl_s, c_s, c_r, q_s, q_r,
):
    r, c = lax.axis_index("row"), lax.axis_index("col")
    zl, x = r // 4, r % 4
    zh, y, k = c // 16, (c // 2) % 8, c % 2

    def dev(x_, y_, zl_, zh_, k_):
        return (zl_ * 4 + x_, zh_ * 16 + y_ * 2 + k_)

    sibling = (r, c + 1 - 2 * k)
    xr, xl = dev((x + 1) % 4, y, zl, zh, k), dev((x + 3) % 4, y, zl, zh, k)
    yr, yl = dev(x, (y + 1) % 8, zl, zh, k), dev(x, (y + 7) % 8, zl, zh, k)

    def remote(src, dst, s, rr, d):
        return pltpu.make_async_remote_copy(
            src_ref=src, dst_ref=dst, send_sem=s, recv_sem=rr, device_id=d, device_id_type=MESH
        )

    def arrived(ref, sem):
        pltpu.make_async_copy(ref, ref, sem).wait()

    bar = pltpu.get_barrier_semaphore()

    def hello(d):
        pl.semaphore_signal(bar, inc=1, device_id=d, device_id_type=MESH)

    @pl.loop(0, 8)
    def _(i):
        hello(dev(x, y, i % 4, (zh + 1 + i // 4) % 3, k))

    me = r * 2 + k

    @pl.loop(1, 32)
    def _(i):
        o = (me + i) % 32
        hello((o // 2, c - k + o % 2))

    hello(yr)
    hello(yl)

    own_b = pltpu.make_async_copy(b_hbm, b_ref.at[k, pl.ds(x * KB, KB)], bl_s)
    own_b.start()
    d = dest[...]
    blk = lax.shift_right_logical(d, 8)
    low = jnp.bitwise_and(d, 255)
    oh = (iota((16, T), 0) == blk).astype(F32)
    before = (iota((T, T), 0) < iota((T, T), 1)).astype(F32).astype(BF)
    cum = jnp.dot(oh.astype(BF), before, preferred_element_type=F32)
    rank = jnp.sum(oh * cum, axis=0, keepdims=True)
    pos = blk * 16 + rank.astype(I32)
    perm = iota((T, T), 0) == pos
    tm = mask[...].astype(F32).astype(BF)
    spread = (lax.shift_right_logical(iota((T, 16), 0), 4) == iota((T, 16), 1)).astype(F32).astype(BF)
    wide = jnp.dot(spread, tm, preferred_element_type=F32)
    keep = jnp.sum(jnp.where(iota(wide.shape, 1) == c, wide, 0.0), axis=1, keepdims=True)
    permf = perm.astype(F32)
    t_ref[...] = jnp.dot((permf * keep).astype(BF), stored[...].astype(BF), preferred_element_type=F32).astype(BF)
    low8 = jnp.broadcast_to(low, (8, T)).astype(F32).astype(BF)
    srow = lax.dot_general(low8, permf.astype(BF), (((1,), (1,)), ((), ())), preferred_element_type=F32)
    slots[r] = srow[:1]
    half = (k * 8 + lax.shift_right_logical(iota((128, 16), 0), 4) == iota((128, 16), 1)).astype(F32).astype(BF)
    pick = (iota((48, 128), 0) == 12 * zl + iota((48, 128), 1)).astype(F32).astype(BF)
    tiles = jnp.dot(half, tm, preferred_element_type=F32).astype(BF)
    w_ref[...] = jnp.dot(tiles, pick, preferred_element_type=F32)

    pl.semaphore_wait(bar, 41)

    away, mine = pl.ds((1 - k) * 128, 128), pl.ds(k * 128, 128)
    to_sib = remote(t_ref.at[away], sib, sib_s.at[0], sib_s.at[1], sibling)
    to_sib.start()
    top, bot = pl.ds(0, HB), pl.ds(HB, HB)

    def bslot(n, xx, h):
        return b_ref.at[n, pl.ds(xx * KB + h * HB, HB)]

    b_out = [
        remote(b_hbm.at[top], bslot(k, x, 0), b_s.at[0], b_r.at[x, 0], xr),
        remote(b_hbm.at[bot], bslot(k, x, 1), b_s.at[1], b_r.at[x, 1], xl),
        remote(b_hbm.at[bot], bslot(k, x, 1), b_s.at[2], b_r.at[x, 1], xr),
        remote(b_hbm.at[top], bslot(k, x, 0), b_s.at[3], b_r.at[x, 0], xl),
    ]
    for cp in b_out:
        cp.start()
    to_sib.wait_recv()
    merged[...] = t_ref[mine] + sib[...]

    j = zh * 8 + y
    tzl, tp = j // 6, j % 6
    a1 = []
    for h in range(NZH):
        self_ = jnp.logical_and(tzl == zl, zh == h)
        cp = remote(merged, a_ref.at[zl, tp], a1_s.at[h], a_r.at[zl, tp], dev(x, y, tzl, h, k))
        a1.append((jnp.logical_not(self_), cp))

        @pl.when(jnp.logical_not(self_))
        def _():
            cp.start()

        @pl.when(self_)
        def _():
            pltpu.make_async_copy(merged, a_ref.at[zl, tp], a_r.at[zl, tp]).start()

    def slot_cp(i):
        o = (r + i) % 16
        return remote(slots.at[r], slots.at[r], q_s, q_r, (o, c))

    @pl.loop(1, 16)
    def _(i):
        slot_cp(i).start()

    xa, xb, xc = (x + 3) % 4, (x + 1) % 4, (x + 2) % 4
    b_sib = []

    def to_sibling(src, xx, h):
        cp = remote(src, bslot(k, xx, h), bs_s.at[len(b_sib)], bs_r.at[xx, h], sibling)
        cp.start()
        b_sib.append(cp)

    arrived(bslot(k, xa, 0), b_r.at[xa, 0])
    relay0 = remote(bslot(k, xa, 0), bslot(k, xa, 0), b_s.at[4], b_r.at[xa, 0], xr)
    relay0.start()
    arrived(bslot(k, xb, 1), b_r.at[xb, 1])
    relay1 = remote(bslot(k, xb, 1), bslot(k, xb, 1), b_s.at[5], b_r.at[xb, 1], xl)
    relay1.start()
    b_out += [relay0, relay1]
    to_sibling(b_hbm.at[top], x, 0)
    to_sibling(b_hbm.at[bot], x, 1)
    to_sibling(bslot(k, xa, 0), xa, 0)
    to_sibling(bslot(k, xb, 1), xb, 1)

    u = (y + 2 * zl) % 8

    def a_cp(q, p, way):
        return remote(a_ref.at[q, p], a_ref.at[q, p], a_s.at[q, p, way], a_r.at[q, p], (yr, yl)[way])

    def reach(p, way):
        far = jnp.where(p >= 3, 1, 0)
        return 3 + far if way == 0 else 4 - far

    def ring(q, s, waits=False):
        for way in ((0, 1) if s else (0,)):
            p = (u - s + 8 * way + 8 - 8 * way) % 8 if way == 0 else (u + s) % 8
            valid = p < NP
            if s:
                valid = jnp.logical_and(valid, s <= reach(p, way))

            @pl.when(valid)
            def _():
                if not waits:
                    arrived(a_ref.at[q, p], a_r.at[q, p])
                for w in ((way,) if s else (0, 1)):
                    if s >= 4:
                        continue

                    @pl.when(s < reach(p, w))
                    def _():
                        if waits:
                            a_cp(q, p, w).wait_send()
                        else:
                            a_cp(q, p, w).start()

    def c_send(q, i, act):
        o, n = k * 8 + i % 8, i // 8
        src = c_tx.at[q * 16 + i]
        dst = c_rx.at[zl, q * 4 + x]
        self_ = jnp.logical_and(o == r, n == k)

        @pl.when(jnp.logical_not(self_))
        def _():
            remote(src, dst, c_s, c_r, (o, c - k + n)).start()

        @pl.when(self_)
        def _():
            pltpu.make_async_copy(src, dst, c_r).start()

    def product(q):
        w = w_ref[...]
        for n in range(2):
            acc = jnp.zeros((128, T), F32)
            for p in range(NP):
                a = a_ref[q, p]
                for e in range(2):
                    keep_ = w[:, 2 * p + e : 2 * p + e + 1] > 0.5
                    lhs = jnp.where(keep_, a.astype(F32), 0.0).astype(BF)
                    acc = acc + jnp.dot(lhs, b_ref[n, (2 * p + e) * T : (2 * p + e + 1) * T], preferred_element_type=F32)
            c_tx[q * 16 + n * 8 : q * 16 + n * 8 + 8] = acc.astype(BF).reshape(8, 16, T)

        @pl.loop(0, 16)
        def _(i):
            c_send(q, i, None)

    for step in ORDER:
        if step == "B":
            for xx, h in ((xa, 1), (xb, 0), (xc, 0), (xc, 1)):
                arrived(bslot(k, xx, h), b_r.at[xx, h])
                to_sibling(bslot(k, xx, h), xx, h)
            own_b.wait()
            for xx in range(4):
                for h in range(2):
                    arrived(bslot(1 - k, xx, h), bs_r.at[xx, h])
        elif step[1] is None:
            product(step[0])
        else:
            ring(*step)

    to_sib.wait_send()
    for ok, cp in a1:

        @pl.when(ok)
        def _():
            cp.wait_send()

    for cp in b_out + b_sib:
        cp.wait_send()
    for step in ORDER:
        if step != "B" and step[1] is not None and step[1] < 4:
            ring(*step, waits=True)
    arrived(slots.at[pl.ds(0, 15)], q_s)
    arrived(slots.at[pl.ds(0, 15)], q_r)

    sel = (iota((T, T), 0) == r * 16 + jnp.bitwise_and(iota((T, T), 1), 15)).astype(F32).astype(BF)
    g = jnp.dot(slots[...].reshape(16, T).astype(BF), sel, preferred_element_type=F32)
    own = lax.shift_right_logical(iota((16, T), 1), 4) == iota((16, T), 0)
    at = jnp.sum(jnp.where(own, g, 0.0), axis=0, keepdims=True).astype(I32)
    place = (iota((T, T), 0) == at).astype(F32).astype(BF)

    arrived(c_rx, c_r)
    total = jnp.zeros((T, T), F32)
    for g in range(NZL):
        total = total + jnp.dot(place, c_rx[g].reshape(T, T), preferred_element_type=F32)
    out[...] = total / den[...]

    has_own = (r // 8) == k

    @pl.when(has_own)
    def _():
        arrived(c_tx.at[pl.ds(0, 60)], c_s)

    @pl.when(jnp.logical_not(has_own))
    def _():
        arrived(c_tx, c_s)


def local(stored, destination, tile_mask, integrals, denominators):
    vm = pl.BlockSpec(memory_space=pltpu.VMEM)
    dma = pltpu.SemaphoreType.DMA
    return pl.pallas_call(
        kernel,
        out_shape=jax.ShapeDtypeStruct((T, T), F32),
        in_specs=[vm, vm, vm, pl.BlockSpec(memory_space=pl.ANY), vm],
        out_specs=vm,
        scratch_shapes=[
            pltpu.VMEM((T, T), BF),
            pltpu.VMEM((128, T), BF),
            pltpu.VMEM((128, T), BF),
            pltpu.VMEM((4, NP, 128, T), BF),
            pltpu.VMEM((2, 4 * KB, T), BF),
            pltpu.VMEM((64, 16, T), BF),
            pltpu.VMEM((4, 16, 16, T), BF),
            pltpu.VMEM((16, 1, T), F32),
            pltpu.VMEM((128, 128), F32),
            dma((2,)),
            dma((3,)),
            dma((4, NP, 2)),
            dma((4, NP)),
            dma((6,)),
            dma((4, 2)),
            dma((8,)),
            dma((4, 2)),
            dma,
            dma,
            dma,
            dma,
            dma,
        ],
        compiler_params=pltpu.CompilerParams(
            collective_id=0, has_side_effects=True, vmem_limit_bytes=40 << 20
        ),
        name="ladder",
    )(stored, destination.reshape(1, T), tile_mask, integrals, denominators)


def solution(mesh):
    return jax.shard_map(
        local,
        mesh=mesh,
        in_specs=(P("row", "col"), P("row"), P(), P("row", "col"), P("row", "col")),
        out_specs=P("row", "col"),
        check_vma=False,
    )
```

```python
import jax
import jax.numpy as jnp
from jax import lax
from jax.experimental import pallas as pl
from jax.experimental.pallas import tpu as pltpu
from jax.sharding import PartitionSpec as P

MESH = pl.DeviceIdType.MESH
BF, F32, I32 = jnp.bfloat16, jnp.float32, jnp.int32
NX, NY, NZL, NZH = 4, 8, 4, 3
T = 256
KB = 768
HB = KB // 2
NP = 6
PACE = 0.6
EXTRA = {(0, 1): "B1", (0, 2): "B2", (0, 3): "B3"}
ORDER = []
for _, _s, _t in sorted((s + PACE * t, s, t) for t in range(4) for s in range(5)):
    ORDER += [EXTRA[_t, _s]] if (_t, _s) in EXTRA else []
    ORDER.append((_t, _s))
    if _s == 4:
        ORDER += (["B4"] if _t == 0 else []) + [(_t, None)]


def iota(shape, dim):
    return lax.broadcasted_iota(I32, shape, dim)


def shr(a, n):
    return lax.shift_right_logical(a, n)


def first_row(block):
    xx = jnp.bitwise_and(block, 3)
    return jnp.bitwise_and(xx, 1) * 128 + shr(block, 2) * 32 + shr(xx, 1) * 16


def block_of(row):
    return jnp.bitwise_and(shr(row, 5), 3) * 4 + jnp.bitwise_and(shr(row, 4), 1) * 2 + shr(row, 7)


def kernel(
    stored_h, dest_h, mask_h, b_hbm, den_h, out,
    stored, dest, mask, den, in_s, t_ref, sib, merged, a_ref, b_ref, c_tx, c_rx, slots, w_ref,
    sib_s, a1_s, a_s, a_r, b_s, b_r, bs_s, bs_r, bl_s, c_s, c_r, q_s, q_r,
):
    r, c = lax.axis_index("row"), lax.axis_index("col")
    zl, x = r // 4, r % 4
    zh, y, k = c // 16, (c // 2) % 8, c % 2

    def dev(x_, y_, zl_, zh_, k_):
        return (zl_ * 4 + x_, zh_ * 16 + y_ * 2 + k_)

    sibling = (r, c + 1 - 2 * k)
    xr, xl = dev((x + 1) % 4, y, zl, zh, k), dev((x + 3) % 4, y, zl, zh, k)
    yr, yl = dev(x, (y + 1) % 8, zl, zh, k), dev(x, (y + 7) % 8, zl, zh, k)

    def remote(src, dst, s, rr, d):
        return pltpu.make_async_remote_copy(
            src_ref=src, dst_ref=dst, send_sem=s, recv_sem=rr, device_id=d, device_id_type=MESH
        )

    def arrived(ref, sem):
        pltpu.make_async_copy(ref, ref, sem).wait()

    ins = [
        pltpu.make_async_copy(src, dst, in_s.at[i])
        for i, (src, dst) in enumerate(((dest_h, dest), (mask_h, mask), (stored_h, stored), (den_h, den)))
    ]
    for cp in ins:
        cp.start()
    bar = pltpu.get_barrier_semaphore()

    def hello(d):
        pl.semaphore_signal(bar, inc=1, device_id=d, device_id_type=MESH)

    @pl.loop(0, 8)
    def _(i):
        hello(dev(x, y, i % 4, (zh + 1 + i // 4) % 3, k))

    me = r * 2 + k

    @pl.loop(1, 32)
    def _(i):
        o = (me + i) % 32
        hello((o // 2, c - k + o % 2))

    hello(yr)
    hello(yl)

    own_b = pltpu.make_async_copy(b_hbm, b_ref.at[k, pl.ds(x * KB, KB)], bl_s)
    own_b.start()
    ins[0].wait()
    d = dest[...]
    blk = shr(d, 8)
    low = jnp.bitwise_and(d, 255)
    oh = (iota((16, T), 0) == blk).astype(F32)
    before = (iota((T, T), 0) < iota((T, T), 1)).astype(F32).astype(BF)
    cum = jnp.dot(oh.astype(BF), before, preferred_element_type=F32)
    rank = jnp.sum(oh * cum, axis=0, keepdims=True)
    pos = first_row(blk) + rank.astype(I32)
    perm = iota((T, T), 0) == pos
    ins[1].wait()
    tm = mask[...].astype(F32).astype(BF)
    spread = (block_of(iota((T, 16), 0)) == iota((T, 16), 1)).astype(F32).astype(BF)
    wide = jnp.dot(spread, tm, preferred_element_type=F32)
    keep = jnp.sum(jnp.where(iota(wide.shape, 1) == c, wide, 0.0), axis=1, keepdims=True)
    permf = perm.astype(F32)
    ins[2].wait()
    t_ref[...] = jnp.dot((permf * keep).astype(BF), stored[...].astype(BF), preferred_element_type=F32).astype(BF)
    low8 = jnp.broadcast_to(low, (8, T)).astype(F32).astype(BF)
    srow = lax.dot_general(low8, permf.astype(BF), (((1,), (1,)), ((), ())), preferred_element_type=F32)
    slots[r] = srow[:1]
    row = iota((512, 16), 0)
    half = (shr(row, 7) * 4 + jnp.bitwise_and(shr(row, 4), 1) * 2 + k == iota((512, 16), 1)).astype(F32).astype(BF)
    pick = (iota((48, 128), 0) == 12 * zl + iota((48, 128), 1)).astype(F32).astype(BF)
    tiles = jnp.dot(half, tm, preferred_element_type=F32).astype(BF)
    w_ref[...] = jnp.dot(tiles, pick, preferred_element_type=F32)

    pl.semaphore_wait(bar, 41)

    away, mine = pl.ds((1 - k) * 128, 128), pl.ds(k * 128, 128)
    to_sib = remote(t_ref.at[away], sib, sib_s.at[0], sib_s.at[1], sibling)
    to_sib.start()
    top, bot = pl.ds(0, HB), pl.ds(HB, HB)

    def bslot(n, xx, h):
        return b_ref.at[n, pl.ds(xx * KB + h * HB, HB)]

    b_out = [
        remote(b_hbm.at[top], bslot(k, x, 0), b_s.at[0], b_r.at[x, 0], xr),
        remote(b_hbm.at[bot], bslot(k, x, 1), b_s.at[1], b_r.at[x, 1], xl),
        remote(b_hbm.at[bot], bslot(k, x, 1), b_s.at[2], b_r.at[x, 1], xr),
        remote(b_hbm.at[top], bslot(k, x, 0), b_s.at[3], b_r.at[x, 0], xl),
    ]
    for cp in b_out:
        cp.start()
    to_sib.wait_recv()
    merged[...] = t_ref[mine] + sib[...]

    j = zh * 8 + y
    tzl, tp = j // 6, j % 6
    def a1_self(h):
        return jnp.logical_and(tzl == zl, zh == h)

    for t in range(4):
        for h in range(NZH):
            src, dst = merged.at[pl.ds(t * 32, 32)], a_ref.at[t, tp, zl]

            @pl.when(jnp.logical_not(a1_self(h)))
            def _():
                remote(src, dst, a1_s.at[h], a_r.at[t, tp], dev(x, y, tzl, h, k)).start()

            @pl.when(a1_self(h))
            def _():
                pltpu.make_async_copy(src, dst, a_r.at[t, tp]).start()

    def slot_cp(i):
        o = (r + i) % 16
        return remote(slots.at[r], slots.at[r], q_s, q_r, (o, c))

    @pl.loop(1, 16)
    def _(i):
        slot_cp(i).start()

    xa, xb, xc = (x + 3) % 4, (x + 1) % 4, (x + 2) % 4
    b_sib = []

    def to_sibling(src, xx, h):
        cp = remote(src, bslot(k, xx, h), bs_s.at[len(b_sib)], bs_r.at[xx, h], sibling)
        cp.start()
        b_sib.append(cp)

    arrived(bslot(k, xa, 0), b_r.at[xa, 0])
    relay0 = remote(bslot(k, xa, 0), bslot(k, xa, 0), b_s.at[4], b_r.at[xa, 0], xr)
    relay0.start()
    arrived(bslot(k, xb, 1), b_r.at[xb, 1])
    relay1 = remote(bslot(k, xb, 1), bslot(k, xb, 1), b_s.at[5], b_r.at[xb, 1], xl)
    relay1.start()
    b_out += [relay0, relay1]

    u = (y + 2 * zl) % 8

    def a_cp(q, p, way):
        return remote(a_ref.at[q, p], a_ref.at[q, p], a_s.at[q, p, way], a_r.at[q, p], (yr, yl)[way])

    def reach(p, way):
        far = jnp.where(p >= 3, 1, 0)
        return 3 + far if way == 0 else 4 - far

    def ring(q, s, waits=False):
        for way in ((0, 1) if s else (0,)):
            p = (u - s + 8 * way + 8 - 8 * way) % 8 if way == 0 else (u + s) % 8
            valid = p < NP
            if s:
                valid = jnp.logical_and(valid, s <= reach(p, way))

            @pl.when(valid)
            def _():
                if not waits:
                    arrived(a_ref.at[q, p], a_r.at[q, p])
                for w in ((way,) if s else (0, 1)):
                    if s >= 4:
                        continue

                    @pl.when(s < reach(p, w))
                    def _():
                        if waits:
                            a_cp(q, p, w).wait_send()
                        else:
                            a_cp(q, p, w).start()

    def c_send(t, n, xh):
        o = t * 4 + xh * 2 + k
        src, dst = c_tx.at[t * 4 + n * 2 + xh], c_rx.at[zl, x]
        self_ = jnp.logical_and(o == r, n == k)

        @pl.when(jnp.logical_not(self_))
        def _():
            remote(src, dst, c_s, c_r, (o, c - k + n)).start()

        @pl.when(self_)
        def _():
            pltpu.make_async_copy(src, dst, c_r).start()

    def product(t):
        w = w_ref[t * 128 : (t + 1) * 128]
        for n in range(2):
            acc = jnp.zeros((128, T), F32)
            for p in range(NP):
                a = a_ref[t, p].reshape(128, T)
                for e in range(2):
                    keep_ = w[:, 2 * p + e : 2 * p + e + 1] > 0.5
                    lhs = jnp.where(keep_, a.astype(F32), 0.0).astype(BF)
                    acc = acc + jnp.dot(lhs, b_ref[n, (2 * p + e) * T : (2 * p + e + 1) * T], preferred_element_type=F32)
            acc = acc.astype(BF).reshape(4, 2, 16, T)
            for xh in range(2):
                c_tx[t * 4 + n * 2 + xh] = acc[:, xh]
                c_send(t, n, xh)

    for step in ORDER:
        if step == "B1":
            to_sibling(b_hbm.at[top], x, 0)
            to_sibling(b_hbm.at[bot], x, 1)
            to_sibling(bslot(k, xa, 0), xa, 0)
            to_sibling(bslot(k, xb, 1), xb, 1)
        elif step == "B2":
            for xx, h in ((xa, 1), (xb, 0)):
                arrived(bslot(k, xx, h), b_r.at[xx, h])
                to_sibling(bslot(k, xx, h), xx, h)
        elif step == "B3":
            for xx, h in ((xc, 0), (xc, 1)):
                arrived(bslot(k, xx, h), b_r.at[xx, h])
                to_sibling(bslot(k, xx, h), xx, h)
        elif step == "B4":
            own_b.wait()
            for xx in range(4):
                for h in range(2):
                    arrived(bslot(1 - k, xx, h), bs_r.at[xx, h])
        elif step[1] is None:
            product(step[0])
        else:
            ring(*step)

    to_sib.wait_send()
    for h in range(NZH):

        @pl.when(jnp.logical_not(a1_self(h)))
        def _():
            arrived(merged, a1_s.at[h])

    for cp in b_out + b_sib:
        cp.wait_send()
    for step in ORDER:
        if step[0] != "B" and step[1] is not None and step[1] < 4:
            ring(*step, waits=True)
    arrived(slots.at[pl.ds(0, 15)], q_s)
    arrived(slots.at[pl.ds(0, 15)], q_r)

    sel = (iota((T, T), 0) == first_row(r) + jnp.bitwise_and(iota((T, T), 1), 15)).astype(F32).astype(BF)
    g = jnp.dot(slots[...].reshape(16, T).astype(BF), sel, preferred_element_type=F32)
    lane = iota((16, T), 1)
    own = jnp.bitwise_and(shr(lane, 4), 3) * 4 + shr(lane, 6) == iota((16, T), 0)
    at = jnp.sum(jnp.where(own, g, 0.0), axis=0, keepdims=True).astype(I32)
    place = (iota((T, T), 0) == at).astype(F32).astype(BF)

    ins[3].wait()
    arrived(c_rx, c_r)
    total = jnp.zeros((T, T), F32)
    for g in range(NZL):
        total = total + jnp.dot(place, c_rx[g].reshape(T, T), preferred_element_type=F32)
    out[...] = total / den[...]

    has_own = x % 2 == k

    @pl.when(has_own)
    def _():
        arrived(c_tx.at[pl.ds(0, 15)], c_s)

    @pl.when(jnp.logical_not(has_own))
    def _():
        arrived(c_tx, c_s)


def local(stored, destination, tile_mask, integrals, denominators):
    vm = pl.BlockSpec(memory_space=pltpu.VMEM)
    dma = pltpu.SemaphoreType.DMA
    return pl.pallas_call(
        kernel,
        out_shape=jax.ShapeDtypeStruct((T, T), F32),
        in_specs=[pl.BlockSpec(memory_space=pltpu.HBM)] * 5,
        out_specs=vm,
        scratch_shapes=[
            pltpu.VMEM((T, T), F32),
            pltpu.VMEM((1, T), I32),
            pltpu.VMEM((16, 48), I32),
            pltpu.VMEM((T, T), F32),
            dma((4,)),
            pltpu.VMEM((T, T), BF),
            pltpu.VMEM((128, T), BF),
            pltpu.VMEM((128, T), BF),
            pltpu.VMEM((4, NP, 4, 32, T), BF),
            pltpu.VMEM((2, 4 * KB, T), BF),
            pltpu.VMEM((16, 4, 16, T), BF),
            pltpu.VMEM((4, 4, 4, 16, T), BF),
            pltpu.VMEM((16, 1, T), F32),
            pltpu.VMEM((512, 128), F32),
            dma((2,)),
            dma((3,)),
            dma((4, NP, 2)),
            dma((4, NP)),
            dma((6,)),
            dma((4, 2)),
            dma((8,)),
            dma((4, 2)),
            dma,
            dma,
            dma,
            dma,
            dma,
        ],
        compiler_params=pltpu.CompilerParams(
            collective_id=0, has_side_effects=True, vmem_limit_bytes=62 << 20
        ),
        name="ladder",
    )(stored, destination.reshape(1, T), tile_mask, integrals, denominators)


def solution(mesh):
    return jax.shard_map(
        local,
        mesh=mesh,
        in_specs=(P("row", "col"), P("row"), P(), P("row", "col"), P("row", "col")),
        out_specs=P("row", "col"),
        check_vma=False,
    )
```

```python
import jax
import jax.numpy as jnp
from jax import lax
from jax.experimental import pallas as pl
from jax.experimental.pallas import tpu as pltpu
from jax.sharding import PartitionSpec as P

MESH = pl.DeviceIdType.MESH
BF, F32, I32 = jnp.bfloat16, jnp.float32, jnp.int32
NX, NY, NZL, NZH = 4, 8, 4, 3
T = 256
KB = 768
HB = KB // 2
NP = 6
PACE = 0.7
EXTRA = {(0, 1): "B1", (0, 2): "B2", (0, 3): "B3"}
LATER = {(0, 0): ["A2"], (1, 0): ["A3"]}
ORDER = []
for _, _s, _t in sorted((s + PACE * t, s, t) for t in range(4) for s in range(5)):
    ORDER += [EXTRA[_t, _s]] if (_t, _s) in EXTRA else []
    ORDER.append((_t, _s))
    ORDER += LATER.get((_t, _s), [])
    if _s == 4:
        ORDER += (["B4"] if _t == 0 else []) + [(_t, None)]


def iota(shape, dim):
    return lax.broadcasted_iota(I32, shape, dim)


def shr(a, n):
    return lax.shift_right_logical(a, n)


def first_row(block):
    xx = jnp.bitwise_and(block, 3)
    chunk = jnp.bitwise_xor(shr(block, 2), shr(xx, 1))
    return jnp.bitwise_and(xx, 1) * 128 + chunk * 32 + shr(xx, 1) * 16


def target(chunk, xh, core):
    return jnp.bitwise_xor(chunk, xh) * 4 + xh * 2 + core


def block_of(row):
    return target(jnp.bitwise_and(shr(row, 5), 3), jnp.bitwise_and(shr(row, 4), 1), shr(row, 7))


def kernel(
    stored_h, dest_h, mask_h, b_hbm, den_h, out,
    stored, dest, mask, den, in_s, t_ref, sib, merged, a_ref, b_ref, c_tx, c_rx, slots, slot_out, w_ref,
    sib_s, a1_s, a_s, a_r, b_s, b_r, bs_s, bs_r, bl_s, c_s, c_r, q_s, q_r,
):
    r, c = lax.axis_index("row"), lax.axis_index("col")
    zl, x = r // 4, r % 4
    zh, y, k = c // 16, (c // 2) % 8, c % 2

    def dev(x_, y_, zl_, zh_, k_):
        return (zl_ * 4 + x_, zh_ * 16 + y_ * 2 + k_)

    sibling = (r, c + 1 - 2 * k)
    xr, xl = dev((x + 1) % 4, y, zl, zh, k), dev((x + 3) % 4, y, zl, zh, k)
    yr, yl = dev(x, (y + 1) % 8, zl, zh, k), dev(x, (y + 7) % 8, zl, zh, k)

    def remote(src, dst, s, rr, d):
        return pltpu.make_async_remote_copy(
            src_ref=src, dst_ref=dst, send_sem=s, recv_sem=rr, device_id=d, device_id_type=MESH
        )

    def arrived(ref, sem):
        pltpu.make_async_copy(ref, ref, sem).wait()

    ins = [
        pltpu.make_async_copy(src, dst, in_s.at[i])
        for i, (src, dst) in enumerate(((dest_h, dest), (mask_h, mask), (stored_h, stored), (den_h, den)))
    ]
    for cp in ins:
        cp.start()
    bar = pltpu.get_barrier_semaphore()

    def hello(d):
        pl.semaphore_signal(bar, inc=1, device_id=d, device_id_type=MESH)

    j, u = zh * 8 + y, (y + 2 * zl) % 8
    tzl, tp = j // NP, j % NP
    for d in (sibling, xr, xl, yr, yl):
        hello(d)

    src_zh = (NP * zl + u) // 8

    @pl.when(u < NP)
    def _():
        for q in range(NZL):

            @pl.when(jnp.logical_not(jnp.logical_and(q == zl, src_zh == zh)))
            def _():
                hello(dev(x, y, q, src_zh, k))

    giver = x % 2

    @pl.loop(0, 16)
    def _(i):
        @pl.when(jnp.logical_or(i != r, giver != k))
        def _():
            hello((i, c - k + giver))

    greeted = 5 + NZH - (tzl == zl).astype(I32) + 16 - (giver == k).astype(I32)

    own_b = pltpu.make_async_copy(b_hbm, b_ref.at[k, pl.ds(x * KB, KB)], bl_s)
    own_b.start()
    ins[0].wait()
    d = dest[...]
    blk = shr(d, 8)
    low = jnp.bitwise_and(d, 255)
    oh = (iota((16, T), 0) == blk).astype(F32)
    before = (iota((T, T), 0) < iota((T, T), 1)).astype(F32).astype(BF)
    cum = jnp.dot(oh.astype(BF), before, preferred_element_type=F32)
    rank = jnp.sum(oh * cum, axis=0, keepdims=True)
    pos = first_row(blk) + rank.astype(I32)
    perm = iota((T, T), 0) == pos
    ins[1].wait()
    tm = mask[...].astype(F32).astype(BF)
    spread = (block_of(iota((T, 16), 0)) == iota((T, 16), 1)).astype(F32).astype(BF)
    wide = jnp.dot(spread, tm, preferred_element_type=F32)
    keep = jnp.sum(jnp.where(iota(wide.shape, 1) == c, wide, 0.0), axis=1, keepdims=True)
    sorting = (perm.astype(F32) * keep).astype(BF)
    ins[2].wait()
    t_ref[...] = jnp.dot(sorting, stored[...].astype(BF), preferred_element_type=F32).astype(BF)

    pl.semaphore_wait(bar, greeted)

    away, mine = pl.ds((1 - k) * 128, 128), pl.ds(k * 128, 128)
    to_sib = remote(t_ref.at[away], sib, sib_s.at[0], sib_s.at[1], sibling)
    to_sib.start()
    top, bot = pl.ds(0, HB), pl.ds(HB, HB)

    def bslot(n, xx, h):
        return b_ref.at[n, pl.ds(xx * KB + h * HB, HB)]

    b_out = [
        remote(b_hbm.at[top], bslot(k, x, 0), b_s.at[0], b_r.at[x, 0], xr),
        remote(b_hbm.at[bot], bslot(k, x, 1), b_s.at[1], b_r.at[x, 1], xl),
        remote(b_hbm.at[bot], bslot(k, x, 1), b_s.at[2], b_r.at[x, 1], xr),
        remote(b_hbm.at[top], bslot(k, x, 0), b_s.at[3], b_r.at[x, 0], xl),
    ]
    for cp in b_out:
        cp.start()
    to_sib.wait_recv()
    merged[...] = t_ref[mine] + sib[...]

    def a1_self(h):
        return jnp.logical_and(tzl == zl, zh == h)

    def a1_send(t):
        for h in range(NZH):
            src, dst = merged.at[pl.ds(t * 32, 32)], a_ref.at[t, tp, zl]

            @pl.when(jnp.logical_not(a1_self(h)))
            def _():
                remote(src, dst, a1_s.at[h], a_r.at[t, tp], dev(x, y, tzl, h, k)).start()

            @pl.when(a1_self(h))
            def _():
                pltpu.make_async_copy(src, dst, a_r.at[t, tp]).start()

    for t in range(2):
        a1_send(t)

    low8 = jnp.broadcast_to(low, (8, T)).astype(F32).astype(BF)
    srow = lax.dot_general(low8, perm.astype(F32).astype(BF), (((1,), (1,)), ((), ())), preferred_element_type=F32)
    slot_out[0] = srow[:1]
    row = iota((512, 16), 0)
    half = (target(shr(row, 7), jnp.bitwise_and(shr(row, 4), 1), k) == iota((512, 16), 1)).astype(F32).astype(BF)
    pick = (iota((48, 128), 0) == 12 * zl + iota((48, 128), 1)).astype(F32).astype(BF)
    tiles = jnp.dot(half, tm, preferred_element_type=F32).astype(BF)
    w_ref[...] = jnp.dot(tiles, pick, preferred_element_type=F32)

    @pl.loop(0, 16)
    def _(i):
        o, n = i // 4 * 4 + i // 2 % 2 * 2 + k, i % 2
        self_ = jnp.logical_and(o == r, n == k)

        @pl.when(jnp.logical_not(self_))
        def _():
            remote(slot_out.at[0], slots.at[r], q_s, q_r, (o, c - k + n)).start()

        @pl.when(self_)
        def _():
            pltpu.make_async_copy(slot_out.at[0], slots.at[r], q_r).start()

    xa, xb, xc = (x + 3) % 4, (x + 1) % 4, (x + 2) % 4
    b_sib = []

    def to_sibling(src, xx, h):
        cp = remote(src, bslot(k, xx, h), bs_s.at[len(b_sib)], bs_r.at[xx, h], sibling)
        cp.start()
        b_sib.append(cp)

    arrived(bslot(k, xa, 0), b_r.at[xa, 0])
    relay0 = remote(bslot(k, xa, 0), bslot(k, xa, 0), b_s.at[4], b_r.at[xa, 0], xr)
    relay0.start()
    arrived(bslot(k, xb, 1), b_r.at[xb, 1])
    relay1 = remote(bslot(k, xb, 1), bslot(k, xb, 1), b_s.at[5], b_r.at[xb, 1], xl)
    relay1.start()
    b_out += [relay0, relay1]

    def part(i, p):
        return a_ref.at[i, p]

    def a_cp(i, p, way):
        return remote(part(i, p), part(i, p), a_s.at[i, p, way], a_r.at[i, p], (yr, yl)[way])

    def reach(p, way):
        far = jnp.where(p >= 3, 1, 0)
        return 3 + far if way == 0 else 4 - far

    def ring(i, s, waits=False):
        for way in ((0, 1) if s else (0,)):
            p = jnp.bitwise_and(u + (8 - s if way == 0 else s), 7)
            valid = p < NP
            if s:
                valid = jnp.logical_and(valid, s <= reach(p, way))

            @pl.when(valid)
            def _():
                if not waits:
                    arrived(part(i, p), a_r.at[i, p])
                for w in ((way,) if s else (0, 1)):
                    if s >= 4:
                        continue

                    @pl.when(s < reach(p, w))
                    def _():
                        if waits:
                            a_cp(i, p, w).wait_send()
                        else:
                            a_cp(i, p, w).start()

    def c_send(t, n, xh):
        o = target(t, xh, k)
        src, dst = c_tx.at[t * 4 + n * 2 + xh], c_rx.at[zl, x]
        self_ = jnp.logical_and(o == r, n == k)

        @pl.when(jnp.logical_not(self_))
        def _():
            remote(src, dst, c_s, c_r, (o, c - k + n)).start()

        @pl.when(self_)
        def _():
            pltpu.make_async_copy(src, dst, c_r).start()

    def product(t):
        w = w_ref[t * 128 : (t + 1) * 128]
        for n in range(2):
            acc = jnp.zeros((128, T), F32)
            for p in range(NP):
                a = a_ref[t, p].reshape(128, T)
                for e in range(2):
                    keep_ = w[:, 2 * p + e : 2 * p + e + 1] > 0.5
                    lhs = jnp.where(keep_, a.astype(F32), 0.0).astype(BF)
                    acc = acc + jnp.dot(lhs, b_ref[n, (2 * p + e) * T : (2 * p + e + 1) * T], preferred_element_type=F32)
            acc = acc.astype(BF).reshape(4, 2, 16, T)
            for xh in range(2):
                c_tx[t * 4 + n * 2 + xh] = acc[:, xh]
                c_send(t, n, xh)

    for step in ORDER:
        if step[0] == "A":
            a1_send(int(step[1]))
        elif step == "B1":
            to_sibling(b_hbm.at[top], x, 0)
            to_sibling(b_hbm.at[bot], x, 1)
            to_sibling(bslot(k, xa, 0), xa, 0)
            to_sibling(bslot(k, xb, 1), xb, 1)
        elif step == "B2":
            for xx, h in ((xa, 1), (xb, 0)):
                arrived(bslot(k, xx, h), b_r.at[xx, h])
                to_sibling(bslot(k, xx, h), xx, h)
        elif step == "B3":
            for xx, h in ((xc, 0), (xc, 1)):
                arrived(bslot(k, xx, h), b_r.at[xx, h])
                to_sibling(bslot(k, xx, h), xx, h)
        elif step == "B4":
            own_b.wait()
            for xx in range(4):
                for h in range(2):
                    arrived(bslot(1 - k, xx, h), bs_r.at[xx, h])
        elif step[1] is None:
            product(step[0])
        else:
            ring(*step)

    to_sib.wait_send()
    for h in range(NZH):

        @pl.when(jnp.logical_not(a1_self(h)))
        def _():
            arrived(merged, a1_s.at[h])

    for cp in b_out + b_sib:
        cp.wait_send()
    for step in ORDER:
        if step[0] not in ("A", "B") and step[1] is not None and step[1] < 4:
            ring(*step, waits=True)
    arrived(slots, q_r)

    sel = (iota((T, T), 0) == first_row(r) + jnp.bitwise_and(iota((T, T), 1), 15)).astype(F32).astype(BF)
    g = jnp.dot(slots[...].reshape(16, T).astype(BF), sel, preferred_element_type=F32)
    lane = iota((16, T), 1)
    own = jnp.bitwise_and(shr(lane, 4), 3) * 4 + shr(lane, 6) == iota((16, T), 0)
    at = jnp.sum(jnp.where(own, g, 0.0), axis=0, keepdims=True).astype(I32)
    place = (iota((T, T), 0) == at).astype(F32).astype(BF)

    ins[3].wait()
    arrived(c_rx, c_r)
    total = jnp.zeros((T, T), F32)
    for g in range(NZL):
        total = total + jnp.dot(place, c_rx[g].reshape(T, T), preferred_element_type=F32)
    out[...] = total / den[...]

    has_own = x % 2 == k

    @pl.when(has_own)
    def _():
        arrived(c_tx.at[pl.ds(0, 15)], c_s)
        arrived(slots.at[pl.ds(0, 15)], q_s)

    @pl.when(jnp.logical_not(has_own))
    def _():
        arrived(c_tx, c_s)
        arrived(slots, q_s)


def local(stored, destination, tile_mask, integrals, denominators):
    vm = pl.BlockSpec(memory_space=pltpu.VMEM)
    dma = pltpu.SemaphoreType.DMA
    return pl.pallas_call(
        kernel,
        out_shape=jax.ShapeDtypeStruct((T, T), F32),
        in_specs=[pl.BlockSpec(memory_space=pltpu.HBM)] * 5,
        out_specs=vm,
        scratch_shapes=[
            pltpu.VMEM((T, T), F32),
            pltpu.VMEM((1, T), I32),
            pltpu.VMEM((16, 48), I32),
            pltpu.VMEM((T, T), F32),
            dma((4,)),
            pltpu.VMEM((T, T), BF),
            pltpu.VMEM((128, T), BF),
            pltpu.VMEM((128, T), BF),
            pltpu.VMEM((4, NP, 4, 32, T), BF),
            pltpu.VMEM((2, 4 * KB, T), BF),
            pltpu.VMEM((16, 4, 16, T), BF),
            pltpu.VMEM((4, 4, 4, 16, T), BF),
            pltpu.VMEM((16, 1, T), F32),
            pltpu.VMEM((1, 1, T), F32),
            pltpu.VMEM((512, 128), F32),
            dma((2,)),
            dma((3,)),
            dma((4, NP, 2)),
            dma((4, NP)),
            dma((6,)),
            dma((4, 2)),
            dma((8,)),
            dma((4, 2)),
            dma,
            dma,
            dma,
            dma,
            dma,
        ],
        compiler_params=pltpu.CompilerParams(
            collective_id=0, has_side_effects=True, vmem_limit_bytes=62 << 20
        ),
        name="ladder",
    )(stored, destination.reshape(1, T), tile_mask, integrals, denominators)


def solution(mesh):
    return jax.shard_map(
        local,
        mesh=mesh,
        in_specs=(P("row", "col"), P("row"), P(), P("row", "col"), P("row", "col")),
        out_specs=P("row", "col"),
        check_vma=False,
    )
```
